512 devices in a mesh: expert: 32 (over y_hi, z), dp: 16 (over x, y_lo, core).
Axes of the slice: x: 4, y: 8 (y_hi: 4, y_lo: 2; y = y_hi * 2 + y_lo), z: 8, core: 2. Of those that a mesh axis runs over, the one named last changes fastest.
Arguments:
- tokens: bfloat16 [65536, 2560], P(('expert', 'dp')), may hold values from -6 to 6
- cotangent: bfloat16 [65536, 2560], P(('expert', 'dp')), may hold values from -6 to 6
- gates: bfloat16 [65536, 2], P(('expert', 'dp')), may hold values from 0.099609375 to 1
- routes: int32 [65536, 2], P(('expert', 'dp')), may hold values from -1 to 7, as said below
- gate_proj: bfloat16 [32, 192, 2560], P('expert', 'dp'), may hold values from -0.125 to 0.125
- up_proj: bfloat16 [32, 192, 2560], P('expert', 'dp'), may hold values from -0.125 to 0.125
- down_proj: bfloat16 [32, 192, 2560], P('expert', 'dp'), may hold values from -0.21875 to 0.21875
Outputs:
- grad_tokens: bfloat16 [65536, 2560], P(('expert', 'dp'))
- grad_gates: float32 [65536, 2], P(('expert', 'dp'))
- grad_gate_proj: bfloat16 [32, 192, 2560], P('expert', 'dp')
- grad_up_proj: bfloat16 [32, 192, 2560], P('expert', 'dp')
- grad_down_proj: bfloat16 [32, 192, 2560], P('expert', 'dp')
The draws below stay inside these ranges and needn't reach their ends.
Inputs may be any that keep to these rules, and one draw needn't show every extreme that they name: `routes`: each row lists 1 to 2 different experts in its first entries and -1 in the others.
All inputs are finite; a program needn't handle non-finite values.
Results may differ from the reference program's by a relative error of at most 0.0085.
Values may be sent and summed in bfloat16 or wider, within the bound.
A program may use at most 64 MiB of HBM per device.

```python
import math
from functools import partial
import jax
import jax.numpy as jnp
from jax import lax

D = 2560
H = 768
GROUP = 4
KMAX = 2
TOK_DEV = 128
EXPERTS = 8
UNITS = 192
CAP = 16
TOKENS = 65536
N_EXPERT = 32
N_DP = 16


def draw_routes(key, part):
    bias_key, score_key, count_key = jax.random.split(key, 3)
    favour = jax.random.randint(bias_key, (EXPERTS,), 0, 48)
    scores = jax.random.randint(score_key, (TOKENS, EXPERTS), 0, 64) + favour[None, :]
    distinct = scores * EXPERTS + jnp.arange(EXPERTS, dtype=jnp.int32)[None, :]
    top_vals, top_ids = lax.top_k(distinct, KMAX)
    extra = (jax.random.randint(count_key, (TOKENS, 1), 0, 3) == 0).astype(jnp.int32)
    counts = 1 + extra * (KMAX - 1)
    positions = jnp.arange(KMAX, dtype=jnp.int32)[None, :]
    return jnp.where(positions < counts, top_ids, -1).astype(jnp.int32)


def block_scale(rng, dims, cuts, smallest, largest):
    level, own = 1.0, jax.random.fold_in(rng, 6)
    for position, shards_of in cuts:
        draws = jnp.exp(jax.random.uniform(jax.random.fold_in(own, position), (shards_of,), jnp.float32, smallest / len(cuts), largest / len(cuts)))
        level = level * jnp.repeat(draws, dims[position] // shards_of).reshape([-1 if axis == position else 1 for axis in range(len(dims))])
    return level


def bell_draw(stream_key, shape, width, reach, cuts=(), kind=jnp.bfloat16):
    drawn = width * jax.random.normal(stream_key, shape, jnp.float32)
    if cuts:
        drawn = drawn * block_scale(stream_key, shape, cuts, -0.22, 0.18)
    return jnp.clip(drawn, -reach, reach).astype(kind)


def setup_inputs(seed: int = 0) -> dict:
    key_list = jax.random.split(jax.random.key(seed), 8)
    tokens = bell_draw(key_list[0], (TOKENS, D), 1.0, 6.0, ((0, 512),))
    cotangent = bell_draw(key_list[1], (TOKENS, D), 1.0, 6.0, ((0, 512),))
    gates = jnp.clip(jnp.exp(math.log(1.0) - 2.306499 * jax.random.uniform(key_list[2], (TOKENS, KMAX), jnp.float32) ** block_scale(key_list[2], (TOKENS, KMAX), ((0, 512),), -0.2, 0.2)), 0.099609375, 1.0).astype(jnp.bfloat16)
    routes = draw_routes(jax.random.fold_in(key_list[7], 71), 0)
    gate_proj = bell_draw(key_list[4], (N_EXPERT, UNITS, D), D ** -0.5, 0.125, ((0, 32), (1, 16)))
    up_proj = bell_draw(key_list[5], (N_EXPERT, UNITS, D), D ** -0.5, 0.125, ((0, 32), (1, 16)))
    down_proj = bell_draw(key_list[6], (N_EXPERT, UNITS, D), H ** -0.5, 0.21875, ((0, 32), (1, 16)))
    return {"tokens": tokens, "cotangent": cotangent, "gates": gates, "routes": routes, "gate_proj": gate_proj, "up_proj": up_proj, "down_proj": down_proj}


def slot_tables(route_block, experts, capacity):
    expert_range = jnp.arange(experts, dtype=jnp.int32)
    named = route_block[:, :, None] == expert_range[None, None, :]
    hits = jnp.sum(named.astype(jnp.int32), axis=1)
    before = jnp.cumsum(hits, axis=0) - hits
    rank_pick = jnp.sum(jnp.where(named, before[:, None, :], 0), axis=2).astype(jnp.int32)
    kept_slot = (route_block >= 0) & (rank_pick < capacity)
    slot_ids = jnp.where(kept_slot, route_block * capacity + rank_pick, -1).astype(jnp.int32)
    return slot_ids


def unit_pass(rows_x, scaled_dy, gate_rows, up_rows, down_rows):
    contract = (((1,), (1,)), ((), ()))
    pre_gate = lax.dot_general(rows_x, gate_rows, contract, preferred_element_type=jnp.float32)
    pre_up = lax.dot_general(rows_x, up_rows, contract, preferred_element_type=jnp.float32)
    sigmoid_gate = jax.nn.sigmoid(pre_gate)
    activated = pre_gate * sigmoid_gate
    hidden = (activated * pre_up).astype(jnp.bfloat16)
    outward = jnp.dot(hidden, down_rows, preferred_element_type=jnp.float32)
    grad_hidden = lax.dot_general(scaled_dy, down_rows, contract, preferred_element_type=jnp.float32)
    grad_pre_gate = (grad_hidden * pre_up * sigmoid_gate * (1.0 + pre_gate * (1.0 - sigmoid_gate))).astype(jnp.bfloat16)
    grad_pre_up = (grad_hidden * activated).astype(jnp.bfloat16)
    slot_grad = jnp.dot(grad_pre_gate, gate_rows, preferred_element_type=jnp.float32) + jnp.dot(grad_pre_up, up_rows, preferred_element_type=jnp.float32)
    return hidden, grad_pre_gate, grad_pre_up, outward, slot_grad


def reference(tokens, cotangent, gates, routes, gate_proj, up_proj, down_proj):
    slot_count = EXPERTS * CAP
    slot_range = jnp.arange(slot_count, dtype=jnp.int32)
    tok_blocks = tokens.reshape(N_EXPERT, N_DP, TOK_DEV, D)
    cot_blocks = cotangent.reshape(N_EXPERT, N_DP, TOK_DEV, D)
    gate_blocks = gates.reshape(N_EXPERT, N_DP, TOK_DEV, KMAX)
    route_blocks = routes.reshape(N_EXPERT, N_DP, TOK_DEV, KMAX)
    member_ids = jnp.arange(N_EXPERT, dtype=jnp.int32)
    contract_rows = (((0,), (0,)), ((), ()))

    def per_row(grad_sums, row_index):
        source_x = lax.dynamic_index_in_dim(tok_blocks, row_index, axis=1, keepdims=False)
        source_dy = lax.dynamic_index_in_dim(cot_blocks, row_index, axis=1, keepdims=False)
        source_gate = lax.dynamic_index_in_dim(gate_blocks, row_index, axis=1, keepdims=False)
        source_route = lax.dynamic_index_in_dim(route_blocks, row_index, axis=1, keepdims=False)
        slot_ids = jax.vmap(partial(slot_tables, experts=EXPERTS, capacity=CAP))(source_route)
        picked = (slot_ids[:, None, :, :] == slot_range[None, :, None, None]).astype(jnp.float32)
        placing = jnp.sum(picked, axis=3)
        hi = lax.Precision.HIGHEST
        sent_x = jnp.einsum('nst,ntd->nsd', placing, source_x.astype(jnp.float32), precision=hi).astype(jnp.bfloat16)
        sent_dy = jnp.einsum('nst,ntd->nsd', placing, source_dy.astype(jnp.float32), precision=hi).astype(jnp.bfloat16)
        sent_gate = jnp.einsum('nstk,ntk->ns', picked, source_gate.astype(jnp.float32), precision=hi).astype(jnp.bfloat16)
        sent_x = sent_x.reshape(N_EXPERT, EXPERTS, CAP, D)
        sent_dy = sent_dy.reshape(N_EXPERT, EXPERTS, CAP, D)
        sent_gate = sent_gate.reshape(N_EXPERT, EXPERTS, CAP)

        def per_member(operands):
            member, gate_rows, up_rows, down_rows = operands
            expert = member // GROUP
            rows_x = lax.dynamic_index_in_dim(sent_x, expert, axis=1, keepdims=False).reshape(-1, D)
            rows_dy = lax.dynamic_index_in_dim(sent_dy, expert, axis=1, keepdims=False).reshape(-1, D)
            rows_gate = lax.dynamic_index_in_dim(sent_gate, expert, axis=1, keepdims=False).reshape(-1)
            scaled_dy = (rows_gate.astype(jnp.float32)[:, None] * rows_dy.astype(jnp.float32)).astype(jnp.bfloat16)
            hidden, grad_pre_gate, grad_pre_up, outward, slot_grad = unit_pass(rows_x, scaled_dy, gate_rows, up_rows, down_rows)
            gate_part = jnp.sum(rows_dy.astype(jnp.float32) * outward, axis=1).astype(jnp.bfloat16)
            term_gate = lax.dot_general(grad_pre_gate, rows_x, contract_rows, preferred_element_type=jnp.float32)
            term_up = lax.dot_general(grad_pre_up, rows_x, contract_rows, preferred_element_type=jnp.float32)
            term_down = lax.dot_general(hidden, scaled_dy, contract_rows, preferred_element_type=jnp.float32)
            grad_terms = jnp.stack([term_gate, term_up, term_down], axis=0).astype(jnp.bfloat16)
            return slot_grad.astype(jnp.bfloat16), gate_part, grad_terms

        slot_parts, gate_parts, grad_terms = lax.map(per_member, (member_ids, gate_proj, up_proj, down_proj))
        summed = jnp.sum(slot_parts.reshape(EXPERTS, GROUP, N_EXPERT, CAP, D).astype(jnp.float32), axis=1)
        summed = jnp.transpose(summed, (1, 0, 2, 3)).reshape(N_EXPERT, slot_count, D)
        grad_block = jnp.einsum('nst,nsd->ntd', placing, summed, precision=hi).astype(jnp.bfloat16)
        gate_sum = jnp.sum(gate_parts.reshape(EXPERTS, GROUP, N_EXPERT, CAP).astype(jnp.float32), axis=1)
        gate_sum = jnp.transpose(gate_sum, (1, 0, 2)).reshape(N_EXPERT, slot_count)
        gate_block = jnp.einsum('nstk,ns->ntk', picked, gate_sum, precision=hi)
        return grad_sums + grad_terms.astype(jnp.float32), (grad_block, gate_block)

    start_sums = jnp.zeros((N_EXPERT, 3, UNITS, D), jnp.float32)
    grad_sums, outputs = lax.scan(per_row, start_sums, jnp.arange(N_DP, dtype=jnp.int32))
    grad_all, gate_all = outputs
    grad_tokens = jnp.transpose(grad_all, (1, 0, 2, 3)).reshape(TOKENS, D)
    grad_gates = jnp.transpose(gate_all, (1, 0, 2, 3)).reshape(TOKENS, KMAX)
    weight_grads = grad_sums.astype(jnp.bfloat16)
    return grad_tokens, grad_gates, weight_grads[:, 0], weight_grads[:, 1], weight_grads[:, 2]
```

```python
import jax
import jax.numpy as jnp
from jax import lax
from jax.experimental import pallas as pl
from jax.experimental.pallas import tpu as pltpu
from jax.sharding import PartitionSpec as P

D = 2560
EXPERTS = 8
CAP = 16
SOURCES = 32
OWNERS = 16
OWN_UNITS = 12
PAD_UNITS = OWNERS * 16
PACK = 640
PACKED = 3 * 1920
GATE_LANES = 128
WIDE = D + GATE_LANES
MESH = pl.DeviceIdType.MESH
BF = jnp.bfloat16
F32 = jnp.float32

HOPS = ((1, 0), (3, 0), (0, 1), (2, 0), (1, 1), (3, 1), (2, 1))


def flip(bit):
    return 1 - bit


class Place:
    def __init__(self):
        i, d = lax.axis_index("expert"), lax.axis_index("dp")
        self.yh, self.z = lax.div(i, 8), lax.rem(i, 8)
        self.x, self.yl, self.c = lax.div(d, 4), lax.rem(lax.div(d, 2), 2), lax.rem(d, 2)
        self.zh, self.zl = lax.div(self.z, 4), lax.rem(self.z, 4)
        self.xp, self.xh = lax.rem(self.x, 2), lax.div(self.x, 2)
        self.expert = self.yh * 2 + self.zh
        self.near = self.zl + 1 - 2 * lax.rem(self.zl, 2)
        self.far = lax.rem(self.zl + 2, 4)
        self.x_mate = self.dev(x=self.x + 1 - 2 * self.xp)
        self.c_mate = self.dev(c=flip(self.c))
        self.y_side = self.dev(yl=flip(self.yl))
        self.z_far = self.dev(z=self.zh * 4 + self.far)
        self.z_near = self.dev(z=self.zh * 4 + self.near)
        self.x_side = self.dev(x=3 - self.x)

    def dev(self, x=None, yh=None, yl=None, z=None, c=None):
        x = self.x if x is None else x
        yh = self.yh if yh is None else yh
        yl = self.yl if yl is None else yl
        z = self.z if z is None else z
        c = self.c if c is None else c
        return (yh * 8 + z, (x * 2 + yl) * 2 + c)

    def hop(self, dy, dz):
        yh = lax.rem(self.yh + dy, 4)
        zh = flip(self.zh) if dz else self.zh
        return self.dev(yh=yh, z=7 - self.z if dz else self.z), yh * 2 + zh

    def origin(self, dy, dz):
        yh = lax.rem(self.yh + 4 - dy, 4)
        return yh * 2 + (flip(self.zh) if dz else self.zh)

    def owner(self, xh=None, yl=None, zl=None):
        xh = self.xh if xh is None else xh
        yl = self.yl if yl is None else yl
        zl = self.zl if zl is None else zl
        return (xh * 2 + yl) * 4 + zl

    def greet(self):
        barrier = pltpu.get_barrier_semaphore()
        mates = [self.hop(*h)[0] for h in HOPS] + [
            self.x_mate, self.c_mate, self.y_side, self.z_far, self.z_near, self.x_side,
        ]
        for mate in mates:
            pl.semaphore_signal(barrier, inc=1, device_id=mate, device_id_type=MESH)
        pl.semaphore_wait(barrier, len(mates))


class Sends:
    def __init__(self, sems):
        self.sems, self.open = sems, []

    def start(self, src, dst, recv, device):
        copy = pltpu.make_async_remote_copy(
            src_ref=src, dst_ref=dst, send_sem=self.sems.at[len(self.open)], recv_sem=recv,
            device_id=device, device_id_type=MESH,
        )
        copy.start()
        self.open.append(copy)

    def arrived(self, dst, recv, device):
        pltpu.make_async_remote_copy(
            src_ref=dst, dst_ref=dst, send_sem=self.sems.at[0], recv_sem=recv,
            device_id=device, device_id_type=MESH,
        ).wait_recv()

    def finish(self):
        for copy in self.open:
            copy.wait_send()


def spread_kernel(rows_in, w_in, rows, wall, row_sems, w_sems, send_sems, own_sems):
    me = Place()
    me.greet()
    out = Sends(send_sems)
    own_row = (me.c * 2 + me.xp) * 8 + me.expert
    own_w = me.owner()
    keep = [
        pltpu.make_async_copy(rows_in.at[me.expert], rows.at[own_row], own_sems.at[0]),
        pltpu.make_async_copy(w_in, wall.at[own_w], own_sems.at[1]),
    ]

    def slot(c, xp, origin):
        return (c * 2 + xp) * 8 + origin

    def send_row(src, index, device):
        out.start(src, rows.at[index], row_sems.at[index], device)

    def send_w(src, index, devices):
        for device in devices:
            out.start(src, wall.at[index], w_sems.at[index], device)

    def send_hop(hop):
        device, expert = me.hop(*hop)
        send_row(rows_in.at[expert], own_row, device)

    def take_row(hop):
        index = slot(me.c, me.xp, me.origin(*hop))
        out.arrived(rows.at[index], row_sems.at[index], me.c_mate)
        send_row(rows.at[index], index, me.x_mate)
        send_row(rows.at[index], index, me.c_mate)

    def take_mate(hop):
        index = slot(me.c, flip(me.xp), me.origin(*hop))
        out.arrived(rows.at[index], row_sems.at[index], me.c_mate)
        send_row(rows.at[index], index, me.c_mate)

    def take_w(index, devices):
        out.arrived(wall.at[index], w_sems.at[index], me.c_mate)
        send_w(wall.at[index], index, devices)

    own_hop = (0, 0)
    far_w = [me.z_near, me.x_side]
    near_w = [me.x_side]
    send_w(w_in, own_w, [me.y_side, me.z_far])
    send_hop(HOPS[0])
    send_hop(HOPS[1])
    send_row(rows_in.at[me.expert], own_row, me.x_mate)
    send_w(w_in, own_w, far_w)
    for hop in HOPS[2:]:
        send_hop(hop)
    send_row(rows_in.at[me.expert], own_row, me.c_mate)
    for copy in keep:
        copy.start()

    take_w(me.owner(yl=flip(me.yl)), [me.z_far, me.z_near, me.x_side])
    take_row(HOPS[0])
    take_row(HOPS[1])
    take_w(me.owner(zl=me.far), far_w)
    take_w(me.owner(yl=flip(me.yl), zl=me.far), far_w)
    take_row(HOPS[2])
    take_mate(own_hop)
    take_w(me.owner(zl=me.near), near_w)
    take_w(me.owner(zl=me.near, yl=flip(me.yl)), near_w)
    take_row(HOPS[3])
    take_mate(HOPS[0])
    near_far = me.far + 1 - 2 * lax.rem(me.far, 2)
    take_w(me.owner(zl=near_far), near_w)
    take_w(me.owner(zl=near_far, yl=flip(me.yl)), near_w)
    for k in range(4, 7):
        take_row(HOPS[k])
        take_mate(HOPS[k - 3])
    for k in range(4, 7):
        take_mate(HOPS[k])

    def rest_w(zl, carry):
        for yl in range(2):
            index = me.owner(xh=flip(me.xh), yl=yl, zl=zl)
            out.arrived(wall.at[index], w_sems.at[index], me.c_mate)
        return carry

    lax.fori_loop(0, 4, rest_w, 0)

    def rest_row(k, carry):
        index = flip(me.c) * 16 + k
        out.arrived(rows.at[index], row_sems.at[index], me.c_mate)
        return carry

    lax.fori_loop(0, 16, rest_row, 0)
    for copy in keep:
        copy.wait()
    out.finish()


def collect_kernel(
    part, terms, back, shares,
    from_core, from_mate, to_mate, to_home, wx, wn, wf, wy, sn, sf, sy,
    core_sems, mate_sems, home_sems, w_sems, send_sems,
):
    me = Place()
    me.greet()
    out = Sends(send_sems)
    order = ((0, 0),) + HOPS

    def slot(c, xp, origin):
        return (c * 2 + xp) * 8 + origin

    def add_rows(dst, terms_of):
        def step(k, carry):
            cut = pl.ds(pl.multiple_of(k * 384, 128), 384)
            total = terms_of[0][:, cut].astype(F32)
            for term in terms_of[1:]:
                total = total + term[:, cut].astype(F32)
            dst[:, cut] = total.astype(BF)
            return carry

        lax.fori_loop(0, WIDE // 384, step, 0)

    def add_w(dst, terms_of):
        def step(k, carry):
            cut = pl.ds(pl.multiple_of(k * 640, 128), 640)
            total = terms_of[0][:, cut].astype(F32)
            for term in terms_of[1:]:
                total = total + term[:, cut].astype(F32)
            dst[:, cut] = total.astype(BF)
            return carry

        lax.fori_loop(0, PACKED // 640, step, 0)

    far_near = me.far + 1 - 2 * lax.rem(me.far, 2)
    x_order = [(yl, zl) for zl in (me.near, far_near, me.far, me.zl) for yl in (flip(me.yl), me.yl)]

    def send_x(pairs):
        for yl, zl in pairs:
            out.start(
                terms.at[me.owner(xh=flip(me.xh), yl=yl, zl=zl)], wx.at[yl * 4 + zl],
                w_sems.at[yl * 4 + zl], me.x_side,
            )

    def send_core(xp, hops):
        for hop in hops:
            origin = me.origin(*hop)
            index = xp * 8 + origin
            out.start(
                part.at[slot(flip(me.c), xp, origin)], from_core.at[index], core_sems.at[index],
                me.c_mate,
            )

    send_x(x_order[:4])
    send_core(flip(me.xp), order)
    send_x(x_order[4:])
    send_core(me.xp, order)

    def get(ref, sems, index):
        out.arrived(ref.at[index], sems.at[index], me.c_mate)

    def to_x_mate(k):
        origin = me.origin(*order[k])
        index = flip(me.xp) * 8 + origin
        get(from_core, core_sems, index)
        add_rows(to_mate.at[origin], [part.at[slot(me.c, flip(me.xp), origin)], from_core.at[index]])
        out.start(to_mate.at[origin], from_mate.at[origin], mate_sems.at[origin], me.x_mate)

    def send_home(k):
        origin = me.origin(*order[k])
        index = me.xp * 8 + origin
        get(from_core, core_sems, index)
        get(from_mate, mate_sems, origin)
        sums = [part.at[slot(me.c, me.xp, origin)], from_core.at[index], from_mate.at[origin]]
        if k == 0:
            add_rows(back.at[me.expert], sums)
        else:
            add_rows(to_home.at[origin], sums)
            dy, dz = order[k]
            device, expert = me.hop(4 - dy if dy else 0, dz)
            out.start(to_home.at[origin], back.at[me.expert], home_sems.at[me.expert], device)

    def own(yl, zl):
        return terms.at[me.owner(yl=yl, zl=zl)]

    def near_w(k):
        yl, zl = x_order[k]
        index = yl * 4 + zl
        get(wx, w_sems, index)
        there = yl * 2 + lax.div(zl, 2)
        add_w(sn.at[there], [own(yl, zl), wx.at[index]])
        out.start(sn.at[there], wn.at[there], w_sems.at[8 + there], me.z_near)

    def far_w(k):
        yl, zl = x_order[k]
        index, there = yl * 4 + zl, yl * 2 + lax.div(zl, 2)
        get(wx, w_sems, index)
        out.arrived(wn.at[there], w_sems.at[8 + there], me.c_mate)
        add_w(sf.at[yl], [own(yl, zl), wx.at[index], wn.at[there]])
        out.start(sf.at[yl], wf.at[yl], w_sems.at[12 + yl], me.z_far)

    def last_w(k):
        yl, zl = x_order[k]
        index, there = yl * 4 + zl, yl * 2 + lax.div(zl, 2)
        get(wx, w_sems, index)
        out.arrived(wn.at[there], w_sems.at[8 + there], me.c_mate)
        out.arrived(wf.at[yl], w_sems.at[12 + yl], me.c_mate)
        sums = [own(yl, zl), wx.at[index], wn.at[there], wf.at[yl]]
        if k == 6:
            add_w(sy, sums)
            out.start(sy, wy, w_sems.at[14], me.y_side)
        else:
            out.arrived(wy, w_sems.at[14], me.c_mate)
            add_w(shares, sums + [wy])

    for k in range(4):
        to_x_mate(2 * k)
        to_x_mate(2 * k + 1)
        near_w(k)
    for k in range(1, 5):
        send_home(k)
    far_w(4)
    far_w(5)
    for k in range(5, 8):
        send_home(k)
    last_w(6)
    send_home(0)
    last_w(7)
    for hop in HOPS:
        _, expert = me.hop(*hop)
        get(back, home_sems, expert)
    out.finish()


def picks(k):
    row = lax.broadcasted_iota(jnp.int32, (PAD_UNITS, PAD_UNITS), 0)
    col = lax.broadcasted_iota(jnp.int32, (PAD_UNITS, PAD_UNITS), 1)
    lane = row & 15
    wanted = (row - lane) + 12 + (lane & 3)
    return jnp.where((col == wanted) & ((lane >> 2) == k), 1.0, 0.0).astype(BF)


def units_kernel(rows, wall, part, terms, gate_w, up_w, down_w):
    nt = (((1,), (1,)), ((), ()))
    weights = (gate_w, up_w, down_w)
    put = [picks(k) for k in range(3)]
    for m, w in enumerate(weights):
        last = jnp.zeros((PAD_UNITS, PACK), F32)
        for k in range(3):
            start = m * 1920 + k * PACK
            block = wall[:, :, start : start + PACK].reshape(PAD_UNITS, PACK)
            w[:, k * PACK : (k + 1) * PACK] = block
            last = last + jnp.dot(put[k], block, preferred_element_type=F32)
        w[:, 1920:] = last.astype(BF)

    def stack(lo, start, size):
        return rows[:, lo : lo + 16, start : start + size].reshape(SOURCES * CAP, size)

    pre_gate = jnp.zeros((SOURCES * CAP, PAD_UNITS), F32)
    pre_up = jnp.zeros((SOURCES * CAP, PAD_UNITS), F32)
    grad_hidden = jnp.zeros((SOURCES * CAP, PAD_UNITS), F32)
    for k in range(4):
        x = stack(0, k * PACK, PACK)
        cut = slice(k * PACK, (k + 1) * PACK)
        pre_gate += lax.dot_general(x, gate_w[:, cut], nt, preferred_element_type=F32)
        pre_up += lax.dot_general(x, up_w[:, cut], nt, preferred_element_type=F32)
        grad_hidden += lax.dot_general(
            stack(16, k * PACK, PACK), down_w[:, cut], nt, preferred_element_type=F32
        )
    unit = lax.broadcasted_iota(jnp.int32, (SOURCES * CAP, PAD_UNITS), 1)
    real = (unit & 15) < OWN_UNITS
    sig = jax.nn.sigmoid(pre_gate)
    act = pre_gate * sig
    zero = jnp.zeros_like(pre_gate)
    hidden = jnp.where(real, act * pre_up, zero).astype(BF).astype(F32)
    gpg = jnp.where(real, grad_hidden * pre_up * sig * (1.0 + pre_gate * (1.0 - sig)), zero)
    gpu = jnp.where(real, grad_hidden * act, zero)
    gate_part = jnp.sum(hidden * jnp.where(real, grad_hidden, zero), axis=1, keepdims=True)
    part[:, :, D:] = (
        jnp.broadcast_to(gate_part, (SOURCES * CAP, GATE_LANES))
        .astype(BF)
        .reshape(SOURCES, CAP, GATE_LANES)
    )
    gpg_t, gpu_t, hidden_t = gpg.T.astype(BF), gpu.T.astype(BF), hidden.T.astype(BF)
    gpg, gpu = gpg.astype(BF), gpu.astype(BF)
    for k in range(4):
        cut = slice(k * PACK, (k + 1) * PACK)
        grad = jnp.dot(gpg, gate_w[:, cut], preferred_element_type=F32) + jnp.dot(
            gpu, up_w[:, cut], preferred_element_type=F32
        )
        part[:, :, cut] = grad.astype(BF).reshape(SOURCES, CAP, PACK)
    take = [put[k].astype(F32).T.astype(BF) for k in range(3)]
    for m, (left, lo) in enumerate(((gpg_t, 0), (gpu_t, 0), (hidden_t, 16))):
        last = jnp.dot(left, stack(lo, 1920, PACK), preferred_element_type=F32).astype(BF)
        for k in range(3):
            term = jnp.dot(left, stack(lo, k * PACK, PACK), preferred_element_type=F32)
            term = term + jnp.dot(take[k], last, preferred_element_type=F32)
            start = m * 1920 + k * PACK
            terms[:, :, start : start + PACK] = term.astype(BF).reshape(OWNERS, 16, PACK)


def spread(rows_in, w_in):
    anywhere = pl.BlockSpec(memory_space=pl.ANY)
    dma = pltpu.SemaphoreType.DMA
    return pl.pallas_call(
        spread_kernel,
        out_shape=(
            jax.ShapeDtypeStruct((SOURCES, 2 * CAP, D), BF),
            jax.ShapeDtypeStruct((OWNERS, 16, PACKED), BF),
        ),
        in_specs=[anywhere] * 2,
        out_specs=(anywhere, anywhere),
        scratch_shapes=[dma((SOURCES,)), dma((OWNERS,)), dma((46,)), dma((2,))],
        compiler_params=pltpu.CompilerParams(collective_id=0, has_side_effects=True),
        name="spread",
    )(rows_in, w_in)


def units(rows, wall):
    return pl.pallas_call(
        units_kernel,
        out_shape=(
            jax.ShapeDtypeStruct((SOURCES, CAP, WIDE), BF),
            jax.ShapeDtypeStruct((OWNERS, 16, PACKED), BF),
        ),
        in_specs=[pl.BlockSpec(memory_space=pltpu.VMEM)] * 2,
        out_specs=(pl.BlockSpec(memory_space=pltpu.VMEM),) * 2,
        scratch_shapes=[pltpu.VMEM((PAD_UNITS, D), BF)] * 3,
        compiler_params=pltpu.CompilerParams(vmem_limit_bytes=50 * 2**20),
        name="units",
    )(rows, wall)


def collect(part, terms):
    vmem = pl.BlockSpec(memory_space=pltpu.VMEM)
    dma = pltpu.SemaphoreType.DMA
    row, w = (CAP, WIDE), (16, PACKED)
    return pl.pallas_call(
        collect_kernel,
        out_shape=(
            jax.ShapeDtypeStruct((EXPERTS, CAP, WIDE), BF),
            jax.ShapeDtypeStruct((16, PACKED), BF),
        ),
        in_specs=[vmem] * 2,
        out_specs=(vmem, vmem),
        scratch_shapes=[
            pltpu.VMEM((16, *row), BF), pltpu.VMEM((8, *row), BF), pltpu.VMEM((8, *row), BF),
            pltpu.VMEM((8, *row), BF),
            pltpu.VMEM((8, *w), BF), pltpu.VMEM((4, *w), BF), pltpu.VMEM((2, *w), BF),
            pltpu.VMEM(w, BF),
            pltpu.VMEM((4, *w), BF), pltpu.VMEM((2, *w), BF), pltpu.VMEM(w, BF),
            dma((16,)), dma((8,)), dma((8,)), dma((15,)), dma((46,)),
        ],
        compiler_params=pltpu.CompilerParams(
            collective_id=1, has_side_effects=True, vmem_limit_bytes=40 * 2**20
        ),
        name="collect",
    )(part, terms)


def slot_tables(routes):
    named = routes[:, :, None] == jnp.arange(EXPERTS, dtype=jnp.int32)[None, None, :]
    hits = jnp.sum(named.astype(F32), axis=1).astype(BF)
    rows = routes.shape[0]
    earlier = jnp.tri(rows, rows, -1, dtype=BF)
    before = jnp.dot(earlier, hits, preferred_element_type=F32)
    rank = jnp.sum(jnp.where(named, before[:, None, :], 0.0), axis=2).astype(jnp.int32)
    return jnp.where((routes >= 0) & (rank < CAP), routes * CAP + rank, -1)


def pack(w):
    tail = jnp.concatenate([w[4 * k : 4 * k + 4, 1920:] for k in range(3)], axis=1)
    return jnp.concatenate([w[:, :1920], tail], axis=0)


def unpack(packed):
    tail = jnp.concatenate(
        [packed[12:, k * PACK : (k + 1) * PACK] for k in range(3)], axis=0
    )
    return jnp.concatenate([packed[:12, :1920], tail], axis=1)


def per_device(tokens, cotangent, gates, routes, gate_proj, up_proj, down_proj):
    slot_count = EXPERTS * CAP
    slot_ids = slot_tables(routes)
    picked = slot_ids[None, :, :] == jnp.arange(slot_count, dtype=jnp.int32)[:, None, None]
    place = jnp.any(picked, axis=2).astype(BF)
    gate_of = jnp.sum(jnp.where(picked, gates.astype(F32)[None], 0.0), axis=(1, 2))
    sent_x = jnp.dot(place, tokens, preferred_element_type=F32).astype(BF)
    sent_y = jnp.dot(place, cotangent, preferred_element_type=F32)
    scaled = (gate_of[:, None] * sent_y).astype(BF)
    rows_in = jnp.concatenate(
        [sent_x.reshape(EXPERTS, CAP, D), scaled.reshape(EXPERTS, CAP, D)], axis=1
    )
    w_in = jnp.concatenate([pack(gate_proj[0]), pack(up_proj[0]), pack(down_proj[0])], axis=1)
    rows, wall = spread(rows_in, w_in)
    part, terms = units(rows, wall)
    back, shares = collect(part, terms)
    back = back.reshape(slot_count, WIDE)
    grad_tokens = lax.dot_general(
        place, back[:, :D], (((0,), (0,)), ((), ())), preferred_element_type=F32
    ).astype(BF)
    gate_sum = back[:, D].astype(F32)
    grad_gates = (
        jnp.sum(jnp.where(picked, gate_sum[:, None, None], 0.0), axis=0) / gates.astype(F32)
    )
    grads = [unpack(shares[:, m * 1920 : (m + 1) * 1920])[None] for m in range(3)]
    return grad_tokens, grad_gates, *grads


def solution(mesh):
    rows = P(("expert", "dp"), None)
    units_of = P("expert", "dp", None)
    return jax.shard_map(
        per_device,
        mesh=mesh,
        in_specs=(rows, rows, rows, rows, units_of, units_of, units_of),
        out_specs=(rows, rows, units_of, units_of, units_of),
        check_vma=False,
    )
```

```python
import jax
import jax.numpy as jnp
from jax import lax
from jax.experimental import pallas as pl
from jax.experimental.pallas import tpu as pltpu
from jax.sharding import PartitionSpec as P

D = 2560
EXPERTS = 8
CAP = 16
SOURCES = 32
TOK = 128
HALF = 256
OWNERS = 16
OWN_UNITS = 12
PAD_UNITS = OWNERS * 16
PACK = 640
PACKED = 3 * 1920
GATE_LANES = 128
WIDE = D + GATE_LANES
MESH = pl.DeviceIdType.MESH
BF = jnp.bfloat16
F32 = jnp.float32

HOPS = ((1, 0), (3, 0), (0, 1), (2, 0), (1, 1), (3, 1), (2, 1))


def flip(bit):
    return 1 - bit


class Place:
    def __init__(self):
        i, d = lax.axis_index("expert"), lax.axis_index("dp")
        self.yh, self.z = lax.div(i, 8), lax.rem(i, 8)
        self.x, self.yl, self.c = lax.div(d, 4), lax.rem(lax.div(d, 2), 2), lax.rem(d, 2)
        self.zh, self.zl = lax.div(self.z, 4), lax.rem(self.z, 4)
        self.xp, self.xh = lax.rem(self.x, 2), lax.div(self.x, 2)
        self.expert = self.yh * 2 + self.zh
        self.near = self.zl + 1 - 2 * lax.rem(self.zl, 2)
        self.far = lax.rem(self.zl + 2, 4)
        self.x_mate = self.dev(x=self.x + 1 - 2 * self.xp)
        self.c_mate = self.dev(c=flip(self.c))
        self.y_side = self.dev(yl=flip(self.yl))
        self.z_far = self.dev(z=self.zh * 4 + self.far)
        self.z_near = self.dev(z=self.zh * 4 + self.near)
        self.x_side = self.dev(x=3 - self.x)

    def dev(self, x=None, yh=None, yl=None, z=None, c=None):
        x = self.x if x is None else x
        yh = self.yh if yh is None else yh
        yl = self.yl if yl is None else yl
        z = self.z if z is None else z
        c = self.c if c is None else c
        return (yh * 8 + z, (x * 2 + yl) * 2 + c)

    def hop(self, dy, dz):
        yh = lax.rem(self.yh + dy, 4)
        zh = flip(self.zh) if dz else self.zh
        return self.dev(yh=yh, z=7 - self.z if dz else self.z), yh * 2 + zh

    def origin(self, dy, dz):
        yh = lax.rem(self.yh + 4 - dy, 4)
        return yh * 2 + (flip(self.zh) if dz else self.zh)

    def owner(self, xh=None, yl=None, zl=None):
        xh = self.xh if xh is None else xh
        yl = self.yl if yl is None else yl
        zl = self.zl if zl is None else zl
        return (xh * 2 + yl) * 4 + zl

    def signal(self):
        barrier = pltpu.get_barrier_semaphore()
        mates = [self.hop(*h)[0] for h in HOPS] + [
            self.x_mate, self.c_mate, self.y_side, self.z_far, self.z_near, self.x_side,
        ]
        for mate in mates:
            pl.semaphore_signal(barrier, inc=1, device_id=mate, device_id_type=MESH)
        self.mates = len(mates)

    def meet(self):
        pl.semaphore_wait(pltpu.get_barrier_semaphore(), self.mates)


class Sends:
    def __init__(self, sems):
        self.sems, self.open = sems, []

    def start(self, src, dst, recv, device):
        copy = pltpu.make_async_remote_copy(
            src_ref=src, dst_ref=dst, send_sem=self.sems.at[len(self.open)], recv_sem=recv,
            device_id=device, device_id_type=MESH,
        )
        copy.start()
        self.open.append(copy)

    def arrived(self, dst, recv, device):
        pltpu.make_async_remote_copy(
            src_ref=dst, dst_ref=dst, send_sem=self.sems.at[0], recv_sem=recv,
            device_id=device, device_id_type=MESH,
        ).wait_recv()

    def finish(self):
        for copy in self.open:
            copy.wait_send()


def pick_rows(k):
    row = lax.broadcasted_iota(jnp.int32, (PAD_UNITS, PAD_UNITS), 0)
    col = lax.broadcasted_iota(jnp.int32, (PAD_UNITS, PAD_UNITS), 1)
    lane = row & 15
    wanted = (row - lane) + 12 + (lane & 3)
    return jnp.where((col == wanted) & ((lane >> 2) == k), 1.0, 0.0)


def layer_kernel(
    tokens, cotangent, gates, routes, gate_proj, up_proj, down_proj,
    grad_tokens, grad_gates, grad_gate, grad_up, grad_down,
    rows_in, rows, wall, tails, place_t, picked, acc, left, left_t, part, terms,
    from_core, from_mate, to_mate, to_home, back, wx, wn, wf, wy, sn, sf, sy, shares,
    row_sems, gather_sems, core_sems, mate_sems, home_sems, reduce_sems, send_sems,
):
    me = Place()
    me.signal()
    out = Sends(send_sems)
    own_w = me.owner()
    nt = (((1,), (1,)), ((), ()))

    for m, w in enumerate((gate_proj, up_proj, down_proj)):
        whole = w[0].astype(F32)
        tail = jnp.concatenate([whole[4 * k : 4 * k + 4, 1920:] for k in range(3)], axis=1)
        packed = jnp.concatenate([whole[:, :1920], tail], axis=0)
        wall[own_w, :, m * 1920 : (m + 1) * 1920] = packed.astype(BF)
    me.meet()

    def slot(xp, c, origin):
        return (xp * 2 + c) * 8 + origin

    own_row = slot(me.xp, me.c, me.expert)

    def send_row(src, index, device):
        out.start(src, rows.at[index], row_sems.at[index], device)

    def send_w(index, devices):
        for device in devices:
            out.start(wall.at[index], wall.at[index], gather_sems.at[index], device)

    def send_hop(hop):
        device, expert = me.hop(*hop)
        send_row(rows_in.at[expert], own_row, device)

    def take_row(hop):
        index = slot(me.xp, me.c, me.origin(*hop))
        out.arrived(rows.at[index], row_sems.at[index], me.c_mate)
        send_row(rows.at[index], index, me.x_mate)
        send_row(rows.at[index], index, me.c_mate)

    def take_mate(hop):
        index = slot(flip(me.xp), me.c, me.origin(*hop))
        out.arrived(rows.at[index], row_sems.at[index], me.c_mate)
        send_row(rows.at[index], index, me.c_mate)

    def take_w(index, devices):
        out.arrived(wall.at[index], gather_sems.at[index], me.c_mate)
        send_w(index, devices)

    def take_core(xp):
        def step(k, carry):
            index = slot(xp, flip(me.c), k)
            out.arrived(rows.at[index], row_sems.at[index], me.c_mate)
            return carry

        lax.fori_loop(0, 8, step, 0)

    send_w(own_w, [me.y_side, me.z_far, me.z_near, me.x_side])

    lane = lax.broadcasted_iota(jnp.int32, (TOK, TOK), 1)
    row = lax.broadcasted_iota(jnp.int32, (TOK, TOK), 0)
    named = [routes[:, j : j + 1] == lane for j in range(2)]
    hits = jnp.where(named[0] | named[1], 1.0, 0.0)
    earlier = jnp.where(lane < row, 1.0, 0.0).astype(BF)
    before = jnp.dot(earlier, hits.astype(BF), preferred_element_type=F32)
    gate_t = jnp.zeros((TOK, TOK), F32)
    placed = jnp.zeros((TOK, TOK), F32)
    for j in range(2):
        rank = jnp.sum(jnp.where(named[j], before, 0.0), axis=1, keepdims=True).astype(jnp.int32)
        route = routes[:, j : j + 1]
        ids = jnp.where((route >= 0) & (rank < CAP), route * CAP + rank, -1)
        one = jnp.where(ids == lane, 1.0, 0.0)
        picked[j] = one.astype(BF)
        placed = placed + one
        gate_t = gate_t + one * gates[:, j : j + 1].astype(F32)
    place_t[...] = placed.astype(BF)
    place = placed.T.astype(BF)
    gate_of = jnp.sum(gate_t.T, axis=1, keepdims=True)
    for k in range(4):
        cut = slice(k * PACK, (k + 1) * PACK)
        sent_x = jnp.dot(place, tokens[:, cut], preferred_element_type=F32)
        sent_y = jnp.dot(place, cotangent[:, cut], preferred_element_type=F32)
        rows_in[:, :CAP, cut] = sent_x.astype(BF).reshape(EXPERTS, CAP, PACK)
        rows_in[:, CAP:, cut] = (gate_of * sent_y).astype(BF).reshape(EXPERTS, CAP, PACK)

    for hop in HOPS[:2]:
        send_hop(hop)
    send_row(rows_in.at[me.expert], own_row, me.x_mate)
    for hop in HOPS[2:]:
        send_hop(hop)
    send_row(rows_in.at[me.expert], own_row, me.c_mate)
    rows[own_row] = rows_in[me.expert]

    far_w = [me.z_near, me.x_side]
    near_w = [me.x_side]
    near_far = me.far + 1 - 2 * lax.rem(me.far, 2)
    y_not = flip(me.yl)

    def side_w(k):
        take_w(me.owner(xh=flip(me.xh), yl=k // 4, zl=k % 4), [])

    take_w(me.owner(yl=y_not), [me.z_far, me.z_near, me.x_side])
    take_row(HOPS[0])
    take_row(HOPS[1])
    take_w(me.owner(zl=me.far), far_w)
    take_w(me.owner(yl=y_not, zl=me.far), far_w)
    take_row(HOPS[2])
    take_mate((0, 0))
    take_w(me.owner(zl=me.near), near_w)
    take_w(me.owner(zl=me.near, yl=y_not), near_w)
    take_row(HOPS[3])
    take_mate(HOPS[0])
    take_w(me.owner(zl=near_far), near_w)
    take_w(me.owner(zl=near_far, yl=y_not), near_w)
    for k in range(4, 7):
        take_row(HOPS[k])
        take_mate(HOPS[k - 3])
    for k in range(8):
        side_w(k)
    take_mate(HOPS[4])

    put = [pick_rows(k).astype(BF) for k in range(3)]
    for m in range(3):
        last = jnp.zeros((PAD_UNITS, PACK), F32)
        for k in range(3):
            start = m * 1920 + k * PACK
            block = wall[:, :, start : start + PACK].reshape(PAD_UNITS, PACK)
            last = last + jnp.dot(put[k], block, preferred_element_type=F32)
        tails[m] = last.astype(BF)

    def unit_rows(m, k):
        if k == 3:
            return tails[m]
        start = m * 1920 + k * PACK
        return wall[:, :, start : start + PACK].reshape(PAD_UNITS, PACK)

    def forward(xp, k):
        cut = slice(k * PACK, (k + 1) * PACK)
        sources = pl.ds(xp * 16, 16)
        x = rows[sources, :CAP, cut].reshape(HALF, PACK)
        s = rows[sources, CAP:, cut].reshape(HALF, PACK)
        for m, operand in enumerate((x, x, s)):
            product = lax.dot_general(operand, unit_rows(m, k), nt, preferred_element_type=F32)
            if k == 0:
                acc[m] = product
            else:
                acc[m] += product

    def hidden_units(xp):
        unit = lax.broadcasted_iota(jnp.int32, (HALF, PAD_UNITS), 1)
        real = (unit & 15) < OWN_UNITS
        pre_gate, pre_up, grad_hidden = acc[0], acc[1], acc[2]
        sig = jax.nn.sigmoid(pre_gate)
        activated = pre_gate * sig
        zero = jnp.zeros_like(pre_gate)
        hidden = jnp.where(real, activated * pre_up, zero).astype(BF).astype(F32)
        grad_hidden = jnp.where(real, grad_hidden, zero)
        gpg = jnp.where(
            real, grad_hidden * pre_up * sig * (1.0 + pre_gate * (1.0 - sig)), zero
        )
        gpu = jnp.where(real, grad_hidden * activated, zero)
        gate_part = jnp.sum(hidden * grad_hidden, axis=1, keepdims=True)
        part[pl.ds(xp * 16, 16), :, D:] = (
            jnp.broadcast_to(gate_part, (HALF, GATE_LANES)).astype(BF).reshape(16, CAP, GATE_LANES)
        )
        here = pl.ds(pl.multiple_of(xp * HALF, HALF), HALF)
        for m, value in enumerate((gpg, gpu)):
            left[m, here, :] = value.astype(BF)
        for m, value in enumerate((gpg, gpu, hidden)):
            left_t[m, :, here] = value.T.astype(BF)

    take_core(me.xp)
    forward(me.xp, 0)
    take_mate(HOPS[5])
    forward(me.xp, 1)
    forward(me.xp, 2)
    take_mate(HOPS[6])
    forward(me.xp, 3)
    hidden_units(me.xp)
    take_core(flip(me.xp))
    for k in range(4):
        forward(flip(me.xp), k)
    hidden_units(flip(me.xp))

    take = [pick_rows(k).T.astype(BF) for k in range(3)]
    for m, lo in enumerate((0, 0, CAP)):

        def stack(k):
            return rows[:, lo : lo + CAP, k * PACK : (k + 1) * PACK].reshape(2 * HALF, PACK)

        last = jnp.dot(left_t[m], stack(3), preferred_element_type=F32).astype(BF)
        for k in range(3):
            term = jnp.dot(left_t[m], stack(k), preferred_element_type=F32)
            term = term + jnp.dot(take[k], last, preferred_element_type=F32)
            start = m * 1920 + k * PACK
            terms[:, :, start : start + PACK] = term.astype(BF).reshape(OWNERS, 16, PACK)

    x_order = [(yl, zl) for zl in (me.near, near_far, me.far, me.zl) for yl in (y_not, me.yl)]
    for yl, zl in x_order:
        out.start(
            terms.at[me.owner(xh=flip(me.xh), yl=yl, zl=zl)], wx.at[yl * 4 + zl],
            reduce_sems.at[yl * 4 + zl], me.x_side,
        )

    for k in range(4):
        grad = jnp.dot(left[0], unit_rows(0, k), preferred_element_type=F32)
        grad = grad + jnp.dot(left[1], unit_rows(1, k), preferred_element_type=F32)
        part[:, :, k * PACK : (k + 1) * PACK] = grad.astype(BF).reshape(SOURCES, CAP, PACK)

    order = ((0, 0),) + HOPS
    for xp in (flip(me.xp), me.xp):
        for hop in order:
            origin = me.origin(*hop)
            index = xp * 8 + origin
            out.start(
                part.at[slot(xp, flip(me.c), origin)], from_core.at[index], core_sems.at[index],
                me.c_mate,
            )

    def add(dst, terms_of, size):
        def step(k, carry):
            cut = pl.ds(pl.multiple_of(k * size, 128), size)
            total = terms_of[0][:, cut].astype(F32)
            for term in terms_of[1:]:
                total = total + term[:, cut].astype(F32)
            dst[:, cut] = total.astype(dst.dtype)
            return carry

        lax.fori_loop(0, dst.shape[1] // size, step, 0)

    def get(ref, sems, index):
        out.arrived(ref.at[index], sems.at[index], me.c_mate)

    def to_x_mate(k):
        origin = me.origin(*order[k])
        index = flip(me.xp) * 8 + origin
        get(from_core, core_sems, index)
        mine = part.at[slot(flip(me.xp), me.c, origin)]
        add(to_mate.at[origin], [mine, from_core.at[index]], 384)
        out.start(to_mate.at[origin], from_mate.at[origin], mate_sems.at[origin], me.x_mate)

    def send_home(k):
        origin = me.origin(*order[k])
        index = me.xp * 8 + origin
        get(from_core, core_sems, index)
        get(from_mate, mate_sems, origin)
        sums = [part.at[slot(me.xp, me.c, origin)], from_core.at[index], from_mate.at[origin]]
        if k == 0:
            add(back.at[me.expert], sums, 384)
        else:
            add(to_home.at[origin], sums, 384)
            dy, dz = order[k]
            device, _ = me.hop(4 - dy if dy else 0, dz)
            out.start(to_home.at[origin], back.at[me.expert], home_sems.at[me.expert], device)

    def reduce_w(k):
        yl, zl = x_order[k]
        there = yl * 2 + lax.div(zl, 2)
        sums = [terms.at[me.owner(yl=yl, zl=zl)], wx.at[yl * 4 + zl]]
        get(wx, reduce_sems, yl * 4 + zl)
        if k < 4:
            add(sn.at[there], sums, 640)
            out.start(sn.at[there], wn.at[there], reduce_sems.at[8 + there], me.z_near)
            return
        out.arrived(wn.at[there], reduce_sems.at[8 + there], me.c_mate)
        sums.append(wn.at[there])
        if k < 6:
            add(sf.at[yl], sums, 640)
            out.start(sf.at[yl], wf.at[yl], reduce_sems.at[12 + yl], me.z_far)
            return
        out.arrived(wf.at[yl], reduce_sems.at[12 + yl], me.c_mate)
        sums.append(wf.at[yl])
        if k == 6:
            add(sy, sums, 640)
            out.start(sy, wy, reduce_sems.at[14], me.y_side)
        else:
            out.arrived(wy, reduce_sems.at[14], me.c_mate)
            add(shares, sums + [wy], 640)

    for k in range(4):
        to_x_mate(2 * k)
        to_x_mate(2 * k + 1)
        reduce_w(k)
    for k in range(1, 5):
        send_home(k)
    reduce_w(4)
    reduce_w(5)
    for k in range(5, 8):
        send_home(k)
    send_home(0)
    reduce_w(6)

    for hop in HOPS:
        _, expert = me.hop(*hop)
        get(back, home_sems, expert)
    for k in range(4):
        cut = slice(k * PACK, (k + 1) * PACK)
        block = back[:, :, cut].reshape(TOK, PACK)
        grad_tokens[:, cut] = jnp.dot(
            place_t[...], block, preferred_element_type=F32
        ).astype(BF)
    gate_back = back[:, :, D:].reshape(TOK, GATE_LANES)
    for j in range(2):
        gate_sum = jnp.dot(picked[j], gate_back, preferred_element_type=F32)
        grad_gates[:, j : j + 1] = gate_sum[:, :1] / gates[:, j : j + 1].astype(F32)

    reduce_w(7)
    for m, grad in enumerate((grad_gate, grad_up, grad_down)):
        whole = shares[:, m * 1920 : (m + 1) * 1920]
        grad[0, :, :1920] = whole[:OWN_UNITS].astype(BF)
        tail = jnp.concatenate(
            [whole[OWN_UNITS:, k * PACK : (k + 1) * PACK] for k in range(3)], axis=0
        )
        grad[0, :, 1920:] = tail.astype(BF)
    out.finish()


def per_device(tokens, cotangent, gates, routes, gate_proj, up_proj, down_proj):
    vmem = pl.BlockSpec(memory_space=pltpu.VMEM)
    dma = pltpu.SemaphoreType.DMA
    row, w = (CAP, WIDE), (16, PACKED)
    scratch = [
        ((EXPERTS, 2 * CAP, D), BF), ((SOURCES, 2 * CAP, D), BF), ((OWNERS, *w), BF),
        ((3, PAD_UNITS, PACK), BF), ((TOK, TOK), BF), ((2, TOK, TOK), BF),
        ((3, HALF, PAD_UNITS), F32), ((2, 2 * HALF, PAD_UNITS), BF), ((3, PAD_UNITS, 2 * HALF), BF),
        ((SOURCES, *row), BF), ((OWNERS, *w), BF),
        ((16, *row), BF), ((8, *row), BF), ((8, *row), BF), ((8, *row), BF), ((EXPERTS, *row), BF),
        ((8, *w), BF), ((4, *w), BF), ((2, *w), BF), (w, BF),
        ((4, *w), BF), ((2, *w), BF), (w, BF), (w, F32),
    ]
    shape = jax.ShapeDtypeStruct
    weight = shape(gate_proj.shape, BF)
    return pl.pallas_call(
        layer_kernel,
        out_shape=(
            shape(tokens.shape, BF), shape(gates.shape, F32), weight, weight, weight,
        ),
        in_specs=[vmem] * 7,
        out_specs=(vmem,) * 5,
        scratch_shapes=[pltpu.VMEM(*s) for s in scratch]
        + [dma((n,)) for n in (SOURCES, OWNERS, 16, 8, 8, 15, 92)],
        compiler_params=pltpu.CompilerParams(
            collective_id=0, has_side_effects=True, vmem_limit_bytes=56 * 2**20
        ),
        name="layer",
    )(tokens, cotangent, gates, routes, gate_proj, up_proj, down_proj)


def solution(mesh):
    rows = P(("expert", "dp"), None)
    units_of = P("expert", "dp", None)
    return jax.shard_map(
        per_device,
        mesh=mesh,
        in_specs=(rows, rows, rows, rows, units_of, units_of, units_of),
        out_specs=(rows, rows, units_of, units_of, units_of),
        check_vma=False,
    )
```

```python
import jax
import jax.numpy as jnp
from jax import lax
from jax.experimental import pallas as pl
from jax.experimental.pallas import tpu as pltpu
from jax.sharding import PartitionSpec as P

D = 2560
EXPERTS = 8
CAP = 16
SOURCES = 32
TOK = 128
HALF = 256
OWNERS = 16
OWN_UNITS = 12
PAD_UNITS = OWNERS * 16
PACK = 640
PACKED = 3 * 1920
GATE_LANES = 128
WIDE = D + GATE_LANES
MESH = pl.DeviceIdType.MESH
BF = jnp.bfloat16
F32 = jnp.float32

ROW_WINDOW = 3
SHARD_WINDOW = 8
HOPS = ((1, 0), (3, 0), (0, 1), (2, 0), (1, 1), (3, 1), (2, 1))

ORIGINS = ((1, 0), (2, 0), (0, 1), (3, 0), (1, 1), (2, 1), (3, 1))


def flip(bit):
    return 1 - bit


class Place:
    def __init__(self):
        i, d = lax.axis_index("expert"), lax.axis_index("dp")
        self.yh, self.z = lax.div(i, 8), lax.rem(i, 8)
        self.x, self.yl, self.c = lax.div(d, 4), lax.rem(lax.div(d, 2), 2), lax.rem(d, 2)
        self.zh, self.zl = lax.div(self.z, 4), lax.rem(self.z, 4)
        self.xp, self.xh = lax.rem(self.x, 2), lax.div(self.x, 2)
        self.expert = self.yh * 2 + self.zh
        self.near = self.zl + 1 - 2 * lax.rem(self.zl, 2)
        self.far = lax.rem(self.zl + 2, 4)
        self.mirror = 3 - self.zl
        self.z_near = self.dev(z=self.zh * 4 + self.near)
        self.z_far = self.dev(z=self.zh * 4 + self.far)
        self.x_mate = self.dev(x=self.x + 1 - 2 * self.xp)
        self.c_mate = self.dev(c=flip(self.c))
        self.y_side = self.dev(yl=flip(self.yl))
        self.mirror = 3 - self.zl
        self.x_side = self.dev(x=3 - self.x)

    def dev(self, x=None, yh=None, yl=None, z=None, c=None):
        x = self.x if x is None else x
        yh = self.yh if yh is None else yh
        yl = self.yl if yl is None else yl
        z = self.z if z is None else z
        c = self.c if c is None else c
        return (yh * 8 + z, (x * 2 + yl) * 2 + c)

    def hop(self, dy, dz):
        yh = lax.rem(self.yh + dy, 4)
        zh = flip(self.zh) if dz else self.zh
        yl = (self.yl, 0, flip(self.yl), 1)[dy]
        kind = (0, 1 + self.yl, 3, 1 + self.yl)[dy]
        return self.dev(yh=yh, yl=yl, z=7 - self.z if dz else self.z), yh * 2 + zh, kind

    def origin(self, kind, dz):
        z = 7 - self.z if dz else self.z
        if kind == 0:
            return self.dev(z=z)
        if kind == 3:
            return self.dev(yh=lax.rem(self.yh + 2, 4), yl=flip(self.yl), z=z)
        return self.dev(yh=lax.rem(self.yh + 3 + 2 * self.yl, 4), yl=kind - 1, z=z)

    def owner(self, xh=None, yl=None, zl=None):
        xh = self.xh if xh is None else xh
        yl = self.yl if yl is None else yl
        zl = self.zl if zl is None else zl
        return (xh * 2 + yl) * 4 + zl

    def signal(self):
        barrier = pltpu.get_barrier_semaphore()
        mates = [self.hop(*h)[0] for h in HOPS]
        beside = lax.rem(self.yh + 3 + 2 * self.yl, 4)
        mates += [self.dev(yh=beside, z=z) for z in (self.z, 7 - self.z)]
        mates += [
            self.x_mate, self.c_mate, self.y_side, self.z_near, self.z_far, self.x_side,
        ]
        for mate in mates:
            pl.semaphore_signal(barrier, inc=1, device_id=mate, device_id_type=MESH)
        self.mates = len(mates)

    def meet(self):
        pl.semaphore_wait(pltpu.get_barrier_semaphore(), self.mates)


class Sends:
    def __init__(self, sems):
        self.sems, self.open = sems, []

    def start(self, src, dst, recv, device):
        copy = pltpu.make_async_remote_copy(
            src_ref=src, dst_ref=dst, send_sem=self.sems.at[len(self.open)], recv_sem=recv,
            device_id=device, device_id_type=MESH,
        )
        copy.start()
        self.open.append(copy)

    def arrived(self, dst, recv, device):
        pltpu.make_async_remote_copy(
            src_ref=dst, dst_ref=dst, send_sem=self.sems.at[0], recv_sem=recv,
            device_id=device, device_id_type=MESH,
        ).wait_recv()

    def finish(self):
        for copy in self.open:
            copy.wait_send()


def pick_rows(k):
    row = lax.broadcasted_iota(jnp.int32, (PAD_UNITS, PAD_UNITS), 0)
    col = lax.broadcasted_iota(jnp.int32, (PAD_UNITS, PAD_UNITS), 1)
    lane = row & 15
    wanted = (row - lane) + 12 + (lane & 3)
    return jnp.where((col == wanted) & ((lane >> 2) == k), 1.0, 0.0)


def layer_kernel(
    tokens, cotangent, gates, routes, gate_proj, up_proj, down_proj,
    back, slots, shares,
    rows_in, rows, wall, tails, acc, left, left_t, part, terms,
    from_core, from_mate, to_mate, to_home, wx, wy, wn, wf, sy, sn, sf,
    row_sems, gather_sems, core_sems, mate_sems, home_sems, reduce_sems, send_sems,
):
    me = Place()
    me.signal()
    out = Sends(send_sems)
    own_w = me.owner()
    nt = (((1,), (1,)), ((), ()))

    for m, w in enumerate((gate_proj, up_proj, down_proj)):
        whole = w[0].astype(F32)
        tail = jnp.concatenate([whole[4 * k : 4 * k + 4, 1920:] for k in range(3)], axis=1)
        packed = jnp.concatenate([whole[:, :1920], tail], axis=0)
        wall[own_w, :, m * 1920 : (m + 1) * 1920] = packed.astype(BF)
    me.meet()

    def slot(xp, c, kind, dz):
        return (xp * 2 + c) * 8 + kind * 2 + dz

    own_row = slot(me.xp, me.c, 0, 0)

    def send_row(src, index, device):
        out.start(src, rows.at[index], row_sems.at[index], device)

    def send_w(index, devices):
        for device in devices:
            out.start(wall.at[index], wall.at[index], gather_sems.at[index], device)

    def send_hop(hop):
        device, expert, kind = me.hop(*hop)
        send_row(rows_in.at[expert], slot(me.xp, me.c, kind, hop[1]), device)

    def take_row(source):
        index = slot(me.xp, me.c, *source)
        out.arrived(rows.at[index], row_sems.at[index], me.c_mate)
        send_row(rows.at[index], index, me.x_mate)
        send_row(rows.at[index], index, me.c_mate)

    def take_mate(source):
        index = slot(flip(me.xp), me.c, *source)
        out.arrived(rows.at[index], row_sems.at[index], me.c_mate)
        send_row(rows.at[index], index, me.c_mate)

    def take_w(index, devices):
        out.arrived(wall.at[index], gather_sems.at[index], me.c_mate)
        send_w(index, devices)

    def take_core(xp):
        def step(k, carry):
            index = slot(xp, flip(me.c), 0, 0) + k
            out.arrived(rows.at[index], row_sems.at[index], me.c_mate)
            return carry

        lax.fori_loop(0, 8, step, 0)

    send_w(own_w, [me.z_far, me.z_near, me.y_side, me.x_side])

    lane = lax.broadcasted_iota(jnp.int32, (TOK, TOK), 1)
    row = lax.broadcasted_iota(jnp.int32, (TOK, TOK), 0)
    named = [routes[j : j + 1, :] == row for j in range(2)]
    hits = jnp.where(named[0] | named[1], 1.0, 0.0)
    earlier = jnp.where(row < lane, 1.0, 0.0).astype(BF)
    before = jnp.dot(hits.astype(BF), earlier, preferred_element_type=F32)
    gate_of = jnp.zeros((TOK, TOK), F32)
    place = jnp.zeros((TOK, TOK), F32)
    for j in range(2):
        rank = jnp.sum(jnp.where(named[j], before, 0.0), axis=0, keepdims=True).astype(jnp.int32)
        route = routes[j : j + 1, :]
        ids = jnp.where((route >= 0) & (rank < CAP), route * CAP + rank, -1)
        slots[j : j + 1, :] = ids
        one = jnp.where(ids == row, 1.0, 0.0)
        place = place + one
        gate_of = gate_of + one * gates[j : j + 1, :].astype(F32)
    place = place.astype(BF)
    gate_of = jnp.sum(gate_of, axis=1, keepdims=True)
    for k in range(4):
        cut = slice(k * PACK, (k + 1) * PACK)
        sent_x = jnp.dot(place, tokens[:, cut], preferred_element_type=F32)
        sent_y = jnp.dot(place, cotangent[:, cut], preferred_element_type=F32)
        rows_in[:, :CAP, cut] = sent_x.astype(BF).reshape(EXPERTS, CAP, PACK)
        rows_in[:, CAP:, cut] = (gate_of * sent_y).astype(BF).reshape(EXPERTS, CAP, PACK)

    y_not, x_not = flip(me.yl), flip(me.xh)
    pending = list(HOPS)

    def next_hop():
        if pending:
            send_hop(pending.pop(0))

    next_hop()
    send_row(rows_in.at[me.expert], own_row, me.x_mate)
    for _ in range(ROW_WINDOW - 1):
        next_hop()
    send_row(rows_in.at[me.expert], own_row, me.c_mate)
    rows[own_row] = rows_in[me.expert]

    def row(k):
        take_row(ORIGINS[k])
        next_hop()

    def mate(k):
        take_mate(ORIGINS[k - 1] if k else (0, 0))

    def line(k):
        zl = (me.far, me.near, me.mirror)[k]
        take_w(me.owner(zl=zl), [me.z_near] * (k == 0) + [me.y_side, me.x_side])

    def across(k):
        take_w(me.owner(yl=y_not, zl=(me.zl, me.far, me.near, me.mirror)[k]), [me.x_side])

    def side(k):
        take_w(me.owner(xh=x_not, yl=k // 4, zl=k % 4), [])

    line(1)
    line(0)
    across(0)
    row(0)
    mate(0)
    line(2)
    row(1)
    mate(1)
    across(2)
    row(2)
    across(1)
    mate(2)
    row(3)
    across(3)
    mate(3)
    row(4)
    mate(4)
    row(5)
    row(6)
    for k in range(8):
        side(k)
    mate(5)

    put = [pick_rows(k).astype(BF) for k in range(3)]
    for m in range(3):
        last = jnp.zeros((PAD_UNITS, PACK), F32)
        for k in range(3):
            start = m * 1920 + k * PACK
            block = wall[:, :, start : start + PACK].reshape(PAD_UNITS, PACK)
            last = last + jnp.dot(put[k], block, preferred_element_type=F32)
        tails[m] = last.astype(BF)

    def unit_rows(m, k):
        if k == 3:
            return tails[m]
        start = m * 1920 + k * PACK
        return wall[:, :, start : start + PACK].reshape(PAD_UNITS, PACK)

    def forward(xp, k):
        cut = slice(k * PACK, (k + 1) * PACK)
        sources = pl.ds(xp * 16, 16)
        x = rows[sources, :CAP, cut].reshape(HALF, PACK)
        s = rows[sources, CAP:, cut].reshape(HALF, PACK)
        for m, operand in enumerate((x, x, s)):
            product = lax.dot_general(operand, unit_rows(m, k), nt, preferred_element_type=F32)
            if k == 0:
                acc[m] = product
            else:
                acc[m] += product

    def hidden_units(xp):
        unit = lax.broadcasted_iota(jnp.int32, (HALF, PAD_UNITS), 1)
        real = (unit & 15) < OWN_UNITS
        pre_gate, pre_up, grad_hidden = acc[0], acc[1], acc[2]
        sig = jax.nn.sigmoid(pre_gate)
        activated = pre_gate * sig
        zero = jnp.zeros_like(pre_gate)
        hidden = jnp.where(real, activated * pre_up, zero).astype(BF).astype(F32)
        grad_hidden = jnp.where(real, grad_hidden, zero)
        gpg = jnp.where(
            real, grad_hidden * pre_up * sig * (1.0 + pre_gate * (1.0 - sig)), zero
        )
        gpu = jnp.where(real, grad_hidden * activated, zero)
        gate_part = jnp.sum(hidden * grad_hidden, axis=1, keepdims=True)
        part[pl.ds(xp * 16, 16), :, D:] = (
            jnp.broadcast_to(gate_part, (HALF, GATE_LANES)).astype(BF).reshape(16, CAP, GATE_LANES)
        )
        here = pl.ds(pl.multiple_of(xp * HALF, HALF), HALF)
        for m, value in enumerate((gpg, gpu)):
            left[m, here, :] = value.astype(BF)
        for m, value in enumerate((gpg, gpu, hidden)):
            left_t[m, :, here] = value.T.astype(BF)

    take_core(me.xp)
    forward(me.xp, 0)
    mate(6)
    forward(me.xp, 1)
    forward(me.xp, 2)
    mate(7)
    forward(me.xp, 3)
    hidden_units(me.xp)
    take_core(flip(me.xp))
    for k in range(4):
        forward(flip(me.xp), k)
    hidden_units(flip(me.xp))

    take = [pick_rows(k).T.astype(BF) for k in range(3)]
    for m, lo in enumerate((0, 0, CAP)):

        def stack(k):
            return rows[:, lo : lo + CAP, k * PACK : (k + 1) * PACK].reshape(2 * HALF, PACK)

        last = jnp.dot(left_t[m], stack(3), preferred_element_type=F32).astype(BF)
        for k in range(3):
            term = jnp.dot(left_t[m], stack(k), preferred_element_type=F32)
            term = term + jnp.dot(take[k], last, preferred_element_type=F32)
            start = m * 1920 + k * PACK
            terms[:, :, start : start + PACK] = term.astype(BF).reshape(OWNERS, 16, PACK)

    x_order = [(yl, zl) for yl in (y_not, me.yl) for zl in (me.near, me.mirror, me.far, me.zl)]
    unsent = list(x_order)

    def next_shard():
        if unsent:
            yl, zl = unsent.pop(0)
            index = yl * 4 + zl
            out.start(
                terms.at[me.owner(xh=x_not, yl=yl, zl=zl)], wx.at[index], reduce_sems.at[index],
                me.x_side,
            )

    for _ in range(SHARD_WINDOW):
        next_shard()

    for k in range(4):
        grad = jnp.dot(left[0], unit_rows(0, k), preferred_element_type=F32)
        grad = grad + jnp.dot(left[1], unit_rows(1, k), preferred_element_type=F32)
        part[:, :, k * PACK : (k + 1) * PACK] = grad.astype(BF).reshape(SOURCES, CAP, PACK)

    order = ((0, 0),) + ORIGINS
    for xp in (flip(me.xp), me.xp):
        for kind, dz in order:
            index = xp * 8 + kind * 2 + dz
            out.start(
                part.at[slot(xp, flip(me.c), kind, dz)], from_core.at[index], core_sems.at[index],
                me.c_mate,
            )

    def add(dst, terms_of, size):
        def step(k, carry):
            cut = pl.ds(pl.multiple_of(k * size, 128), size)
            total = terms_of[0][:, cut].astype(F32)
            for term in terms_of[1:]:
                total = total + term[:, cut].astype(F32)
            dst[:, cut] = total.astype(dst.dtype)
            return carry

        lax.fori_loop(0, dst.shape[1] // size, step, 0)

    def get(ref, sems, index):
        out.arrived(ref.at[index], sems.at[index], me.c_mate)

    def to_x_mate(k):
        kind, dz = order[k]
        place = kind * 2 + dz
        index = flip(me.xp) * 8 + place
        get(from_core, core_sems, index)
        mine = part.at[slot(flip(me.xp), me.c, kind, dz)]
        add(to_mate.at[place], [mine, from_core.at[index]], 384)
        out.start(to_mate.at[place], from_mate.at[place], mate_sems.at[place], me.x_mate)

    def send_home(k):
        kind, dz = order[k]
        place = kind * 2 + dz
        index = me.xp * 8 + place
        get(from_core, core_sems, index)
        get(from_mate, mate_sems, place)
        sums = [part.at[slot(me.xp, me.c, kind, dz)], from_core.at[index], from_mate.at[place]]
        if k == 0:
            add(back.at[me.expert], sums, 384)
        else:
            add(to_home.at[place], sums, 384)
            out.start(
                to_home.at[place], back.at[me.expert], home_sems.at[me.expert],
                me.origin(kind, dz),
            )

    def reduce_w(k):
        yl, zl = x_order[k]
        index = yl * 4 + zl
        sums = [terms.at[me.owner(yl=yl, zl=zl)], wx.at[index]]
        get(wx, reduce_sems, index)
        next_shard()
        if k < 4:
            add(sy.at[k], sums, 640)
            out.start(sy.at[k], wy.at[zl], reduce_sems.at[8 + zl], me.y_side)
            return
        out.arrived(wy.at[zl], reduce_sems.at[8 + zl], me.c_mate)
        sums.append(wy.at[zl])
        half = lax.div(zl, 2)
        if k < 6:
            add(sn.at[k - 4], sums, 640)
            out.start(sn.at[k - 4], wn.at[half], reduce_sems.at[12 + half], me.z_near)
            return
        out.arrived(wn.at[half], reduce_sems.at[12 + half], me.c_mate)
        sums.append(wn.at[half])
        if k == 6:
            add(sf, sums, 640)
            out.start(sf, wf, reduce_sems.at[14], me.z_far)
        else:
            out.arrived(wf, reduce_sems.at[14], me.c_mate)
            add(shares, sums + [wf], 640)

    for k in range(4):
        to_x_mate(2 * k)
        to_x_mate(2 * k + 1)
        reduce_w(k)
    for k in range(1, 5):
        send_home(k)
    reduce_w(4)
    for k in range(5, 8):
        send_home(k)
    reduce_w(5)
    send_home(0)
    reduce_w(6)
    for hop in HOPS:
        _, expert, _ = me.hop(*hop)
        get(back, home_sems, expert)
    reduce_w(7)
    out.finish()


def settle_kernel(back, slots, shares, gates, grad_tokens, grad_gates, grad_gate, grad_up, grad_down):
    row = lax.broadcasted_iota(jnp.int32, (TOK, TOK), 0)
    place = jnp.zeros((TOK, TOK), F32)
    gate_back = back[:, :, D:].reshape(TOK, GATE_LANES).astype(F32)
    for j in range(2):
        one = jnp.where(slots[j : j + 1, :] == row, 1.0, 0.0)
        place = place + one
        gate_sum = jnp.sum(one * gate_back, axis=0, keepdims=True)
        grad_gates[j : j + 1, :] = gate_sum / gates[j : j + 1, :].astype(F32)
    place_t = place.T.astype(BF)
    for k in range(4):
        cut = slice(k * PACK, (k + 1) * PACK)
        block = back[:, :, cut].reshape(TOK, PACK)
        grad_tokens[:, cut] = jnp.dot(place_t, block, preferred_element_type=F32).astype(BF)
    for m, grad in enumerate((grad_gate, grad_up, grad_down)):
        whole = shares[:, m * 1920 : (m + 1) * 1920]
        grad[0, :, :1920] = whole[:OWN_UNITS].astype(BF)
        tail = jnp.concatenate(
            [whole[OWN_UNITS:, k * PACK : (k + 1) * PACK] for k in range(3)], axis=0
        )
        grad[0, :, 1920:] = tail.astype(BF)


def per_device(tokens, cotangent, gates, routes, gate_proj, up_proj, down_proj):
    vmem = pl.BlockSpec(memory_space=pltpu.VMEM)
    dma = pltpu.SemaphoreType.DMA
    row, w = (CAP, WIDE), (16, PACKED)
    scratch = [
        ((EXPERTS, 2 * CAP, D), BF), ((SOURCES, 2 * CAP, D), BF), ((OWNERS, *w), BF),
        ((3, PAD_UNITS, PACK), BF),
        ((3, HALF, PAD_UNITS), F32), ((2, 2 * HALF, PAD_UNITS), BF), ((3, PAD_UNITS, 2 * HALF), BF),
        ((SOURCES, *row), BF), ((OWNERS, *w), BF),
        ((16, *row), BF), ((8, *row), BF), ((8, *row), BF), ((8, *row), BF),
        ((8, *w), BF), ((4, *w), BF), ((2, *w), BF), (w, BF), ((4, *w), BF), ((2, *w), BF), (w, BF),
    ]
    shape = jax.ShapeDtypeStruct
    weight = shape(gate_proj.shape, BF)
    gates_t, routes_t = gates.T, routes.T
    back, slots, shares = pl.pallas_call(
        layer_kernel,
        out_shape=(
            shape((EXPERTS, *row), BF), shape((2, TOK), jnp.int32), shape(w, F32),
        ),
        in_specs=[vmem] * 7,
        out_specs=(vmem,) * 3,
        scratch_shapes=[pltpu.VMEM(*s) for s in scratch]
        + [dma((n,)) for n in (SOURCES, OWNERS, 16, 8, 8, 15, 92)],
        compiler_params=pltpu.CompilerParams(
            collective_id=0, has_side_effects=True, vmem_limit_bytes=56 * 2**20
        ),
        name="layer",
    )(tokens, cotangent, gates_t, routes_t, gate_proj, up_proj, down_proj)
    grad_tokens, grad_gates, *grads = pl.pallas_call(
        settle_kernel,
        out_shape=(
            shape(tokens.shape, BF), shape((2, TOK), F32), weight, weight, weight,
        ),
        in_specs=[vmem] * 4,
        out_specs=(vmem,) * 5,
        name="settle",
    )(back, slots, shares, gates_t)
    return grad_tokens, grad_gates.T, *grads


def solution(mesh):
    rows = P(("expert", "dp"), None)
    units_of = P("expert", "dp", None)
    return jax.shard_map(
        per_device,
        mesh=mesh,
        in_specs=(rows, rows, rows, rows, units_of, units_of, units_of),
        out_specs=(rows, rows, units_of, units_of, units_of),
        check_vma=False,
    )
```

```python
import jax
import jax.numpy as jnp
from jax import lax
from jax.experimental import pallas as pl
from jax.experimental.pallas import tpu as pltpu
from jax.sharding import PartitionSpec as P

D = 2560
EXPERTS = 8
CAP = 16
SOURCES = 32
TOK = 128
HALF = 256
OWNERS = 16
OWN_UNITS = 12
PAD_UNITS = OWNERS * 16
PACK = 640
PACKED = 3 * 1920
GATE_LANES = 128
WIDE = D + GATE_LANES
MESH = pl.DeviceIdType.MESH
BF = jnp.bfloat16
F32 = jnp.float32

ROW_WINDOW = 3
SHARD_WINDOW = 8
HOPS = ((1, 0), (3, 0), (0, 1), (2, 0), (1, 1), (3, 1), (2, 1))

ORIGINS = ((1, 0), (2, 0), (0, 1), (3, 0), (1, 1), (2, 1), (3, 1))


def flip(bit):
    return 1 - bit


class Place:
    def __init__(self):
        i, d = lax.axis_index("expert"), lax.axis_index("dp")
        self.yh, self.z = lax.div(i, 8), lax.rem(i, 8)
        self.x, self.yl, self.c = lax.div(d, 4), lax.rem(lax.div(d, 2), 2), lax.rem(d, 2)
        self.zh, self.zl = lax.div(self.z, 4), lax.rem(self.z, 4)
        self.xp, self.xh = lax.rem(self.x, 2), lax.div(self.x, 2)
        self.expert = self.yh * 2 + self.zh
        self.near = self.zl + 1 - 2 * lax.rem(self.zl, 2)
        self.far = lax.rem(self.zl + 2, 4)
        self.mirror = 3 - self.zl
        self.z_near = self.dev(z=self.zh * 4 + self.near)
        self.z_far = self.dev(z=self.zh * 4 + self.far)
        self.x_mate = self.dev(x=self.x + 1 - 2 * self.xp)
        self.c_mate = self.dev(c=flip(self.c))
        self.y_side = self.dev(yl=flip(self.yl))
        self.mirror = 3 - self.zl
        self.x_side = self.dev(x=3 - self.x)

    def dev(self, x=None, yh=None, yl=None, z=None, c=None):
        x = self.x if x is None else x
        yh = self.yh if yh is None else yh
        yl = self.yl if yl is None else yl
        z = self.z if z is None else z
        c = self.c if c is None else c
        return (yh * 8 + z, (x * 2 + yl) * 2 + c)

    def hop(self, dy, dz):
        yh = lax.rem(self.yh + dy, 4)
        zh = flip(self.zh) if dz else self.zh
        yl = (self.yl, 0, flip(self.yl), 1)[dy]
        kind = (0, 1 + self.yl, 3, 1 + self.yl)[dy]
        return self.dev(yh=yh, yl=yl, z=7 - self.z if dz else self.z), yh * 2 + zh, kind

    def origin(self, kind, dz):
        z = 7 - self.z if dz else self.z
        if kind == 0:
            return self.dev(z=z)
        if kind == 3:
            return self.dev(yh=lax.rem(self.yh + 2, 4), yl=flip(self.yl), z=z)
        return self.dev(yh=lax.rem(self.yh + 3 + 2 * self.yl, 4), yl=kind - 1, z=z)

    def owner(self, xh=None, yl=None, zl=None):
        xh = self.xh if xh is None else xh
        yl = self.yl if yl is None else yl
        zl = self.zl if zl is None else zl
        return (xh * 2 + yl) * 4 + zl

    def signal(self):
        barrier = pltpu.get_barrier_semaphore()
        mates = [self.hop(*h)[0] for h in HOPS]
        beside = lax.rem(self.yh + 3 + 2 * self.yl, 4)
        mates += [self.dev(yh=beside, z=z) for z in (self.z, 7 - self.z)]
        mates += [
            self.x_mate, self.c_mate, self.y_side, self.z_near, self.z_far, self.x_side,
        ]
        for mate in mates:
            pl.semaphore_signal(barrier, inc=1, device_id=mate, device_id_type=MESH)
        self.mates = len(mates)

    def meet(self):
        pl.semaphore_wait(pltpu.get_barrier_semaphore(), self.mates)


class Sends:
    def __init__(self, sems):
        self.sems, self.open = sems, []

    def start(self, src, dst, recv, device):
        copy = pltpu.make_async_remote_copy(
            src_ref=src, dst_ref=dst, send_sem=self.sems.at[len(self.open)], recv_sem=recv,
            device_id=device, device_id_type=MESH,
        )
        copy.start()
        self.open.append(copy)

    def arrived(self, dst, recv, device):
        pltpu.make_async_remote_copy(
            src_ref=dst, dst_ref=dst, send_sem=self.sems.at[0], recv_sem=recv,
            device_id=device, device_id_type=MESH,
        ).wait_recv()

    def finish(self):
        for copy in self.open:
            copy.wait_send()


def pick_rows(k):
    row = lax.broadcasted_iota(jnp.int32, (PAD_UNITS, PAD_UNITS), 0)
    col = lax.broadcasted_iota(jnp.int32, (PAD_UNITS, PAD_UNITS), 1)
    lane = row & 15
    wanted = (row - lane) + 12 + (lane & 3)
    return jnp.where((col == wanted) & ((lane >> 2) == k), 1.0, 0.0)


def layer_kernel(
    tokens, cotangent, gates, routes, gate_proj, up_proj, down_proj,
    back, slots, shares,
    rows_in, rows, wall, tails, acc, left, left_t, part, terms,
    from_core, from_mate, to_mate, to_home, wx, wy, wn, wf, sy, sn, sf,
    row_sems, gather_sems, core_sems, mate_sems, home_sems, reduce_sems, send_sems,
):
    me = Place()
    me.signal()
    out = Sends(send_sems)
    own_w = me.owner()
    nt = (((1,), (1,)), ((), ()))

    for m, w in enumerate((gate_proj, up_proj, down_proj)):
        whole = w[0].astype(F32)
        tail = jnp.concatenate([whole[4 * k : 4 * k + 4, 1920:] for k in range(3)], axis=1)
        packed = jnp.concatenate([whole[:, :1920], tail], axis=0)
        wall[own_w, :, m * 1920 : (m + 1) * 1920] = packed.astype(BF)
    me.meet()

    def slot(xp, c, kind, dz):
        return (xp * 2 + c) * 8 + kind * 2 + dz

    own_row = slot(me.xp, me.c, 0, 0)

    def send_row(src, index, device):
        out.start(src, rows.at[index], row_sems.at[index], device)

    def send_w(index, devices):
        for device in devices:
            out.start(wall.at[index], wall.at[index], gather_sems.at[index], device)

    def send_hop(hop):
        device, expert, kind = me.hop(*hop)
        send_row(rows_in.at[expert], slot(me.xp, me.c, kind, hop[1]), device)

    def take_row(source):
        index = slot(me.xp, me.c, *source)
        out.arrived(rows.at[index], row_sems.at[index], me.c_mate)
        send_row(rows.at[index], index, me.x_mate)
        send_row(rows.at[index], index, me.c_mate)

    def take_mate(source):
        index = slot(flip(me.xp), me.c, *source)
        out.arrived(rows.at[index], row_sems.at[index], me.c_mate)
        send_row(rows.at[index], index, me.c_mate)

    def take_w(index, devices):
        out.arrived(wall.at[index], gather_sems.at[index], me.c_mate)
        send_w(index, devices)

    def take_core(xp):
        def step(k, carry):
            index = slot(xp, flip(me.c), 0, 0) + k
            out.arrived(rows.at[index], row_sems.at[index], me.c_mate)
            return carry

        lax.fori_loop(0, 8, step, 0)

    send_w(own_w, [me.z_far, me.z_near, me.y_side, me.x_side])

    lane = lax.broadcasted_iota(jnp.int32, (TOK, TOK), 1)
    row = lax.broadcasted_iota(jnp.int32, (TOK, TOK), 0)
    named = [routes[j : j + 1, :] == row for j in range(2)]
    hits = jnp.where(named[0] | named[1], 1.0, 0.0)
    earlier = jnp.where(row < lane, 1.0, 0.0).astype(BF)
    before = jnp.dot(hits.astype(BF), earlier, preferred_element_type=F32)
    gate_of = jnp.zeros((TOK, TOK), F32)
    place = jnp.zeros((TOK, TOK), F32)
    for j in range(2):
        rank = jnp.sum(jnp.where(named[j], before, 0.0), axis=0, keepdims=True).astype(jnp.int32)
        route = routes[j : j + 1, :]
        ids = jnp.where((route >= 0) & (rank < CAP), route * CAP + rank, -1)
        slots[j : j + 1, :] = ids
        one = jnp.where(ids == row, 1.0, 0.0)
        place = place + one
        gate_of = gate_of + one * gates[j : j + 1, :].astype(F32)
    place = place.astype(BF)
    gate_of = jnp.sum(gate_of, axis=1, keepdims=True)
    for k in range(4):
        cut = slice(k * PACK, (k + 1) * PACK)
        sent_x = jnp.dot(place, tokens[:, cut], preferred_element_type=F32)
        sent_y = jnp.dot(place, cotangent[:, cut], preferred_element_type=F32)
        rows_in[:, :CAP, cut] = sent_x.astype(BF).reshape(EXPERTS, CAP, PACK)
        rows_in[:, CAP:, cut] = (gate_of * sent_y).astype(BF).reshape(EXPERTS, CAP, PACK)

    y_not, x_not = flip(me.yl), flip(me.xh)
    pending = list(HOPS)

    def next_hop():
        if pending:
            send_hop(pending.pop(0))

    next_hop()
    send_row(rows_in.at[me.expert], own_row, me.x_mate)
    for _ in range(ROW_WINDOW - 1):
        next_hop()
    send_row(rows_in.at[me.expert], own_row, me.c_mate)
    rows[own_row] = rows_in[me.expert]

    def row(k):
        take_row(ORIGINS[k])
        next_hop()

    def mate(k):
        take_mate(ORIGINS[k - 1] if k else (0, 0))

    def line(k):
        zl = (me.far, me.near, me.mirror)[k]
        take_w(me.owner(zl=zl), [me.z_near] * (k == 0) + [me.y_side, me.x_side])

    def across(k):
        take_w(me.owner(yl=y_not, zl=(me.zl, me.far, me.near, me.mirror)[k]), [me.x_side])

    def side(k):
        take_w(me.owner(xh=x_not, yl=k // 4, zl=k % 4), [])

    line(1)
    line(0)
    across(0)
    row(0)
    mate(0)
    line(2)
    row(1)
    mate(1)
    across(2)
    row(2)
    across(1)
    mate(2)
    row(3)
    across(3)
    mate(3)
    row(4)
    mate(4)
    row(5)
    row(6)
    for k in range(8):
        side(k)
    mate(5)

    put = [pick_rows(k).astype(BF) for k in range(3)]
    for m in range(3):
        last = jnp.zeros((PAD_UNITS, PACK), F32)
        for k in range(3):
            start = m * 1920 + k * PACK
            block = wall[:, :, start : start + PACK].reshape(PAD_UNITS, PACK)
            last = last + jnp.dot(put[k], block, preferred_element_type=F32)
        tails[m] = last.astype(BF)

    def unit_rows(m, k):
        if k == 3:
            return tails[m]
        start = m * 1920 + k * PACK
        return wall[:, :, start : start + PACK].reshape(PAD_UNITS, PACK)

    def forward(xp, k):
        cut = slice(k * PACK, (k + 1) * PACK)
        sources = pl.ds(xp * 16, 16)
        x = rows[sources, :CAP, cut].reshape(HALF, PACK)
        s = rows[sources, CAP:, cut].reshape(HALF, PACK)
        for m, operand in enumerate((x, x, s)):
            product = lax.dot_general(operand, unit_rows(m, k), nt, preferred_element_type=F32)
            if k == 0:
                acc[m] = product
            else:
                acc[m] += product

    def hidden_units(xp):
        unit = lax.broadcasted_iota(jnp.int32, (HALF, PAD_UNITS), 1)
        real = (unit & 15) < OWN_UNITS
        pre_gate, pre_up, grad_hidden = acc[0], acc[1], acc[2]
        sig = jax.nn.sigmoid(pre_gate)
        activated = pre_gate * sig
        zero = jnp.zeros_like(pre_gate)
        hidden = jnp.where(real, activated * pre_up, zero).astype(BF).astype(F32)
        grad_hidden = jnp.where(real, grad_hidden, zero)
        gpg = jnp.where(
            real, grad_hidden * pre_up * sig * (1.0 + pre_gate * (1.0 - sig)), zero
        )
        gpu = jnp.where(real, grad_hidden * activated, zero)
        gate_part = jnp.sum(hidden * grad_hidden, axis=1, keepdims=True)
        part[pl.ds(xp * 16, 16), :, D:] = (
            jnp.broadcast_to(gate_part, (HALF, GATE_LANES)).astype(BF).reshape(16, CAP, GATE_LANES)
        )
        here = pl.ds(pl.multiple_of(xp * HALF, HALF), HALF)
        for m, value in enumerate((gpg, gpu)):
            left[m, here, :] = value.astype(BF)
        for m, value in enumerate((gpg, gpu, hidden)):
            left_t[m, :, here] = value.T.astype(BF)

    take_core(me.xp)
    forward(me.xp, 0)
    mate(6)
    forward(me.xp, 1)
    forward(me.xp, 2)
    mate(7)
    forward(me.xp, 3)
    hidden_units(me.xp)
    take_core(flip(me.xp))
    for k in range(4):
        forward(flip(me.xp), k)
    hidden_units(flip(me.xp))

    take = [pick_rows(k).T.astype(BF) for k in range(3)]
    for m, lo in enumerate((0, 0, CAP)):

        def stack(k):
            return rows[:, lo : lo + CAP, k * PACK : (k + 1) * PACK].reshape(2 * HALF, PACK)

        last = jnp.dot(left_t[m], stack(3), preferred_element_type=F32).astype(BF)
        for k in range(3):
            term = jnp.dot(left_t[m], stack(k), preferred_element_type=F32)
            term = term + jnp.dot(take[k], last, preferred_element_type=F32)
            start = m * 1920 + k * PACK
            terms[:, :, start : start + PACK] = term.astype(BF).reshape(OWNERS, 16, PACK)

    x_order = [(yl, zl) for yl in (y_not, me.yl) for zl in (me.near, me.mirror, me.far, me.zl)]
    unsent = list(x_order)

    def next_shard():
        if unsent:
            yl, zl = unsent.pop(0)
            index = yl * 4 + zl
            out.start(
                terms.at[me.owner(xh=x_not, yl=yl, zl=zl)], wx.at[index], reduce_sems.at[index],
                me.x_side,
            )

    for _ in range(SHARD_WINDOW):
        next_shard()

    for k in range(4):
        grad = jnp.dot(left[0], unit_rows(0, k), preferred_element_type=F32)
        grad = grad + jnp.dot(left[1], unit_rows(1, k), preferred_element_type=F32)
        part[:, :, k * PACK : (k + 1) * PACK] = grad.astype(BF).reshape(SOURCES, CAP, PACK)

    order = ((0, 0),) + ORIGINS
    for xp in (flip(me.xp), me.xp):
        for kind, dz in order:
            index = xp * 8 + kind * 2 + dz
            out.start(
                part.at[slot(xp, flip(me.c), kind, dz)], from_core.at[index], core_sems.at[index],
                me.c_mate,
            )

    def add(dst, terms_of, size):
        def step(k, carry):
            cut = pl.ds(pl.multiple_of(k * size, 128), size)
            total = terms_of[0][:, cut].astype(F32)
            for term in terms_of[1:]:
                total = total + term[:, cut].astype(F32)
            dst[:, cut] = total.astype(dst.dtype)
            return carry

        lax.fori_loop(0, dst.shape[1] // size, step, 0)

    def get(ref, sems, index):
        out.arrived(ref.at[index], sems.at[index], me.c_mate)

    def to_x_mate(k):
        kind, dz = order[k]
        place = kind * 2 + dz
        index = flip(me.xp) * 8 + place
        get(from_core, core_sems, index)
        mine = part.at[slot(flip(me.xp), me.c, kind, dz)]
        add(to_mate.at[place], [mine, from_core.at[index]], 384)
        out.start(to_mate.at[place], from_mate.at[place], mate_sems.at[place], me.x_mate)

    def send_home(k):
        kind, dz = order[k]
        place = kind * 2 + dz
        index = me.xp * 8 + place
        get(from_core, core_sems, index)
        get(from_mate, mate_sems, place)
        sums = [part.at[slot(me.xp, me.c, kind, dz)], from_core.at[index], from_mate.at[place]]
        if k == 0:
            add(back.at[me.expert], sums, 384)
        else:
            add(to_home.at[place], sums, 384)
            out.start(
                to_home.at[place], back.at[me.expert], home_sems.at[me.expert],
                me.origin(kind, dz),
            )

    def reduce_w(k):
        yl, zl = x_order[k]
        index = yl * 4 + zl
        sums = [terms.at[me.owner(yl=yl, zl=zl)], wx.at[index]]
        get(wx, reduce_sems, index)
        next_shard()
        if k < 4:
            add(sy.at[k], sums, 640)
            out.start(sy.at[k], wy.at[zl], reduce_sems.at[8 + zl], me.y_side)
            return
        out.arrived(wy.at[zl], reduce_sems.at[8 + zl], me.c_mate)
        sums.append(wy.at[zl])
        half = lax.div(zl, 2)
        if k < 6:
            add(sn.at[k - 4], sums, 640)
            out.start(sn.at[k - 4], wn.at[half], reduce_sems.at[12 + half], me.z_near)
            return
        out.arrived(wn.at[half], reduce_sems.at[12 + half], me.c_mate)
        sums.append(wn.at[half])
        if k == 6:
            add(sf, sums, 640)
            out.start(sf, wf, reduce_sems.at[14], me.z_far)
        else:
            out.arrived(wf, reduce_sems.at[14], me.c_mate)
            add(shares, sums + [wf], 640)

    for k in range(4):
        to_x_mate(2 * k)
        to_x_mate(2 * k + 1)
    reduce_w(0)
    send_home(1)
    send_home(2)
    reduce_w(1)
    send_home(3)
    send_home(4)
    reduce_w(2)
    send_home(5)
    send_home(6)
    reduce_w(3)
    send_home(7)
    reduce_w(4)
    reduce_w(5)
    send_home(0)
    reduce_w(6)
    for hop in HOPS:
        _, expert, _ = me.hop(*hop)
        get(back, home_sems, expert)
    reduce_w(7)
    out.finish()


def settle_kernel(back, slots, shares, gates, grad_tokens, grad_gates, grad_gate, grad_up, grad_down):
    row = lax.broadcasted_iota(jnp.int32, (TOK, TOK), 0)
    place = jnp.zeros((TOK, TOK), F32)
    gate_back = back[:, :, D:].reshape(TOK, GATE_LANES).astype(F32)
    for j in range(2):
        one = jnp.where(slots[j : j + 1, :] == row, 1.0, 0.0)
        place = place + one
        gate_sum = jnp.sum(one * gate_back, axis=0, keepdims=True)
        grad_gates[j : j + 1, :] = gate_sum / gates[j : j + 1, :].astype(F32)
    place_t = place.T.astype(BF)
    for k in range(4):
        cut = slice(k * PACK, (k + 1) * PACK)
        block = back[:, :, cut].reshape(TOK, PACK)
        grad_tokens[:, cut] = jnp.dot(place_t, block, preferred_element_type=F32).astype(BF)
    for m, grad in enumerate((grad_gate, grad_up, grad_down)):
        whole = shares[:, m * 1920 : (m + 1) * 1920]
        grad[0, :, :1920] = whole[:OWN_UNITS].astype(BF)
        tail = jnp.concatenate(
            [whole[OWN_UNITS:, k * PACK : (k + 1) * PACK] for k in range(3)], axis=0
        )
        grad[0, :, 1920:] = tail.astype(BF)


def per_device(tokens, cotangent, gates, routes, gate_proj, up_proj, down_proj):
    vmem = pl.BlockSpec(memory_space=pltpu.VMEM)
    dma = pltpu.SemaphoreType.DMA
    row, w = (CAP, WIDE), (16, PACKED)
    scratch = [
        ((EXPERTS, 2 * CAP, D), BF), ((SOURCES, 2 * CAP, D), BF), ((OWNERS, *w), BF),
        ((3, PAD_UNITS, PACK), BF),
        ((3, HALF, PAD_UNITS), F32), ((2, 2 * HALF, PAD_UNITS), BF), ((3, PAD_UNITS, 2 * HALF), BF),
        ((SOURCES, *row), BF), ((OWNERS, *w), BF),
        ((16, *row), BF), ((8, *row), BF), ((8, *row), BF), ((8, *row), BF),
        ((8, *w), BF), ((4, *w), BF), ((2, *w), BF), (w, BF), ((4, *w), BF), ((2, *w), BF), (w, BF),
    ]
    shape = jax.ShapeDtypeStruct
    weight = shape(gate_proj.shape, BF)
    gates_t, routes_t = gates.T, routes.T
    back, slots, shares = pl.pallas_call(
        layer_kernel,
        out_shape=(
            shape((EXPERTS, *row), BF), shape((2, TOK), jnp.int32), shape(w, F32),
        ),
        in_specs=[vmem] * 7,
        out_specs=(vmem,) * 3,
        scratch_shapes=[pltpu.VMEM(*s) for s in scratch]
        + [dma((n,)) for n in (SOURCES, OWNERS, 16, 8, 8, 15, 92)],
        compiler_params=pltpu.CompilerParams(
            collective_id=0, has_side_effects=True, vmem_limit_bytes=56 * 2**20
        ),
        name="layer",
    )(tokens, cotangent, gates_t, routes_t, gate_proj, up_proj, down_proj)
    grad_tokens, grad_gates, *grads = pl.pallas_call(
        settle_kernel,
        out_shape=(
            shape(tokens.shape, BF), shape((2, TOK), F32), weight, weight, weight,
        ),
        in_specs=[vmem] * 4,
        out_specs=(vmem,) * 5,
        name="settle",
    )(back, slots, shares, gates_t)
    return grad_tokens, grad_gates.T, *grads


def solution(mesh):
    rows = P(("expert", "dp"), None)
    units_of = P("expert", "dp", None)
    return jax.shard_map(
        per_device,
        mesh=mesh,
        in_specs=(rows, rows, rows, rows, units_of, units_of, units_of),
        out_specs=(rows, rows, units_of, units_of, units_of),
        check_vma=False,
    )
```
